32 devices in a mesh: req: 8 (over y, x, core), exp: 4 (over z).
Axes of the slice: x: 2, y: 2, z: 4, core: 2. Of those that a mesh axis runs over, the one named last changes fastest.
Arguments:
- tokens: bfloat16 [4096, 2048], P(('req', 'exp')), may hold values from -6 to 6
- attn_gain: float32 [2048], replicated, may hold values from 0.1 to 1.9
- w_query: bfloat16 [2048, 2048], P(None, 'exp'), may hold values from -0.25 to 0.25
- w_key: bfloat16 [2048, 2048], P(None, 'exp'), may hold values from -0.125 to 0.125
- w_value: bfloat16 [2048, 2048], P(None, 'exp'), may hold values from -0.125 to 0.125
- w_out: bfloat16 [2048, 2048], P('exp'), may hold values from -0.375 to 0.375
- prefix_cache: bfloat16 [4, 1024, 2, 2048], P(None, 'req', None, 'exp'), may hold values from -205 to 205
- group_of: int32 [8], replicated, may hold values from 0 to 3
- lengths: int32 [8], replicated, may hold values from 1 to 512, 2560 in all
- moe_gain: float32 [2048], replicated, may hold values from 0.1 to 1.9
- w_gate: bfloat16 [32, 2048, 512], P(('req', 'exp')), may hold values from -0.125 to 0.125
- w_up: bfloat16 [32, 2048, 512], P(('req', 'exp')), may hold values from -0.125 to 0.125
- w_down: bfloat16 [32, 512, 2048], P(('req', 'exp')), may hold values from -0.25 to 0.25
- routes: int32 [4096, 8], P(('req', 'exp')), may hold values from 0 to 15, all different within a row; in each aligned block of 128 rows (0 to 127, 128 to 255, ...) at most 72 rows name the same one
- route_weights: float32 [4096, 8], P(('req', 'exp')), may hold values from 0.1 to 0.4
Outputs:
- layer_out: bfloat16 [4096, 2048], P(('req', 'exp'))
The draws below stay inside these ranges and needn't reach their ends.
Inputs may be any that keep to these rules, and one draw needn't show every extreme that they name: `routes`: in the rows of one device no expert is named more than 72 times.
All inputs are finite; a program needn't handle non-finite values.
Results may differ from the reference program's by a relative error of at most 0.017.
Values may be sent and summed in bfloat16 or wider, within the bound.
A program may use at most 192 MiB of HBM per device.

```python
import math
import jax
import jax.numpy as jnp
import numpy as np
from jax import lax

D = 2048
HEADS = 16
HD = 128
FF = 1024
TOP = 8
TOK_DEV = 128
PREFIX = 1024
EXPERTS = 16
GROUPS = 4
SLOTS = 512
ROWS = 4096
CAP = 72
N_REQ = 8
N_EXP = 4


def draw_prefix_cache(key, part):
    base_key = jax.random.fold_in(jax.random.fold_in(key, 11), 0)
    shape = (GROUPS, PREFIX, 2, HEADS * HD)
    base = jnp.clip(jax.random.normal(base_key, shape, jnp.float32), -6.0, 6.0)
    return base.astype(jnp.bfloat16)


def plant(values, key, low, high):
    longest = values.shape.index(max(values.shape))
    spots = []
    for shift in (0, 1):
        where = [jax.random.randint(jax.random.fold_in(key, axis), (), 0, length) for axis, length in enumerate(values.shape)]
        where[longest] = (where[longest] + shift) % values.shape[longest]
        spots.append(tuple(where))
    return values.at[spots[0]].set(low).at[spots[1]].set(high)


def block_levels(key, extent, shards, smallest, top_value):
    factor_of = 1.0
    for axis_at, shards_of in shards:
        heights = jax.random.uniform(jax.random.fold_in(jax.random.fold_in(key, 6), axis_at), (shards_of,), jnp.float32, smallest / len(shards), top_value / len(shards))
        factor_of = factor_of * jnp.repeat(jnp.exp(heights), extent[axis_at] // shards_of).reshape((-1,) + (1,) * (len(extent) - 1 - axis_at))
    return factor_of


def split_up(amount, total, reach, lean):
    loads = [(1 << 20) // math.isqrt(grade ** lean) + 1 for grade in range(2, amount + 1)]
    spare, holding = total - reach - (amount - 1), [1] * (amount - 1)
    while spare > 0:
        free = [i for i in range(amount - 1) if holding[i] < reach]
        mass, left = sum([loads[i] for i in free]), spare
        for i in free:
            extra = min(reach - holding[i], max(1, left * loads[i] // mass), spare)
            holding[i] = holding[i] + extra
            spare = spare - extra
    return np.array([reach] + holding)


def ragged(stream_key, amount, total, most, lean):
    if amount == 2:
        one = jax.random.randint(stream_key, (), max(1, total - most), min(most, total - 1) + 1)
        return jnp.stack([one, total - one])
    sizes = jnp.asarray(split_up(amount, total, most, lean), jnp.int32)
    pairs = (amount - 1) // 2
    source_of, receiver = sizes[1:1 + 2 * pairs:2], sizes[2:2 + 2 * pairs:2]
    slack = jnp.minimum(source_of - 1, most - receiver)
    moved = jax.random.randint(jax.random.fold_in(stream_key, 1), (pairs,), 0, 1 << 20) % (slack + 1)
    sizes = sizes.at[1:1 + 2 * pairs:2].set(source_of - moved).at[2:2 + 2 * pairs:2].set(receiver + moved)
    return sizes[jax.random.permutation(jax.random.fold_in(stream_key, 2), amount)]


def routed_block(key, own, number, rows, number_of, top, reach, slope):
    order = jax.random.permutation(key, number_of)
    packed, ordinary = shares(number_of, rows * top, reach, slope, True), shares(number_of, rows * top, reach, slope, False)
    places = jnp.arange(number_of)

    def named(sizes, offset_by):
        used = int((sizes > 0).sum())
        fixed = max(1, used // 4)
        passed = fixed + (places - fixed + offset_by * (used - fixed)) % max(1, number_of - fixed)
        return jnp.zeros((number_of,), jnp.int32).at[order[jnp.where(places < fixed, places, passed)]].set(jnp.asarray(sizes, jnp.int32))

    sizes = jnp.where(number % 4 == 0, named(packed, number // 4), named(ordinary, number - number // 4 - 1))
    mixed = jax.random.permutation(jax.random.fold_in(own, 3), number_of)
    source_of, taker = mixed[0:number_of // 2 * 2:2], mixed[1:number_of // 2 * 2:2]
    room = jnp.minimum(sizes[source_of] - 1, reach - sizes[taker]) // 2
    room = jnp.where((source_of == order[0]) | (taker == order[0]) | (sizes[taker] == 0), 0, jnp.maximum(room, 0))
    passed = jax.random.randint(jax.random.fold_in(own, 4), (number_of // 2,), 0, 1 << 20) % (room + 1)
    sizes = sizes.at[source_of].add(-passed).at[taker].add(passed)
    items = jnp.searchsorted(jnp.cumsum(sizes), jnp.arange(rows * top), side="right").astype(jnp.int32)
    listing = items.reshape(top, rows).T
    listing = listing[jax.random.permutation(jax.random.fold_in(own, 1), rows)]
    offset_by = jax.random.randint(jax.random.fold_in(own, 2), (rows, 1), 0, top)
    return jnp.take_along_axis(listing, (jnp.arange(top)[None, :] + offset_by) % top, axis=1)


def shares(count, total, bound, skew, full):
    loads = [(1 << 20) // math.isqrt(rank ** skew) + 1 for rank in range(1, count + 1)]
    largest = bound if full else min(bound, max(-(-total // count), total * loads[0] // sum(loads)))
    least = 1 if total - largest >= count - 1 else 0
    given, surplus = [largest] + [least] * (count - 1), total - largest - least * (count - 1)
    while surplus > 0:
        candidates = [i for i in range(1, count) if given[i] < largest] or [i for i in range(1, count) if given[i] < bound]
        whole, left = sum([loads[i] for i in candidates]), surplus
        for i in candidates:
            more = min(bound - given[i], max(1, left * loads[i] // whole), surplus)
            given[i] = given[i] + more
            surplus = surplus - more
    return np.array(given)


def noise(own_key, dims, deviation, bound, cuts=(), kind=jnp.bfloat16):
    factor_of = block_levels(own_key, dims, cuts, -0.22, 0.18) if cuts else 1.0
    values = jax.random.normal(own_key, dims, jnp.float32) * deviation * factor_of
    return jnp.minimum(jnp.maximum(values, -bound), bound).astype(kind)


def setup_inputs(seed: int = 0) -> dict:
    arg_keys = jax.random.split(jax.random.key(seed), 16)
    tokens = noise(arg_keys[0], (ROWS, D), 1.0, 6.0, ((0, 32),))
    attn_gain = jnp.clip(1.0 + 0.18 * jax.random.normal(arg_keys[1], (D,), jnp.float32), 0.1, 1.9)
    w_query = noise(arg_keys[2], (D, HEADS * HD), (D // 4) ** -0.5, 0.25, ((1, 4),))
    w_key = noise(arg_keys[3], (D, HEADS * HD), D ** -0.5, 0.125, ((1, 4),))
    w_value = noise(arg_keys[4], (D, HEADS * HD), D ** -0.5, 0.125, ((1, 4),))
    w_out = noise(arg_keys[5], (HEADS * HD, D), (HEADS * HD // 8) ** -0.5, 0.375, ((0, 4),))
    prefix_cache = draw_prefix_cache(jax.random.fold_in(arg_keys[15], 71), 0)
    group_of = plant(jax.random.randint(arg_keys[7], (N_REQ,), 0, GROUPS), jax.random.fold_in(arg_keys[7], 1), 0, GROUPS - 1).astype(jnp.int32)
    lengths = ragged(arg_keys[8], N_REQ, N_REQ * SLOTS * 5 // 8, SLOTS, 2).astype(jnp.int32)
    moe_gain = jnp.clip(1.0 + 0.18 * jax.random.normal(arg_keys[9], (D,), jnp.float32), 0.1, 1.9)
    w_gate = noise(arg_keys[10], (2 * EXPERTS, D, FF // 2), D ** -0.5, 0.125, ((0, 32),))
    w_up = noise(arg_keys[11], (2 * EXPERTS, D, FF // 2), D ** -0.5, 0.125, ((0, 32),))
    w_down = noise(arg_keys[12], (2 * EXPERTS, FF // 2, D), (FF // 2) ** -0.5, 0.25, ((0, 32),))
    routes_keys = jax.random.split(jax.random.fold_in(arg_keys[13], 1), ROWS // TOK_DEV)
    routes_turns = jax.random.permutation(jax.random.fold_in(arg_keys[13], 3), ROWS // TOK_DEV)
    routes = jax.vmap(lambda own, number: routed_block(jax.random.fold_in(arg_keys[13], 2), own, number, TOK_DEV, EXPERTS, TOP, CAP, 1))(routes_keys, routes_turns).reshape((ROWS, TOP))
    route_weights = jnp.clip(0.1 + 0.3 * jax.random.uniform(arg_keys[14], (ROWS, TOP), jnp.float32) ** block_levels(arg_keys[14], (ROWS, TOP), ((0, 32),), -0.2, 0.2), 0.1, 0.4)
    return {"tokens": tokens, "attn_gain": attn_gain, "w_query": w_query, "w_key": w_key, "w_value": w_value, "w_out": w_out, "prefix_cache": prefix_cache, "group_of": group_of, "lengths": lengths, "moe_gain": moe_gain, "w_gate": w_gate, "w_up": w_up, "w_down": w_down, "routes": routes, "route_weights": route_weights}


def norm_rows(values, gain):
    wide = values.astype(jnp.float32)
    return wide * lax.rsqrt(lax.optimization_barrier(jnp.mean(wide * wide, axis=-1, keepdims=True)) + 1e-05) * gain

def rotate(vectors, places):
    half = vectors.shape[-1] // 2
    freqs = 10000.0 ** (-(jnp.arange(half, dtype=jnp.float32) * 2.0) / vectors.shape[-1])
    angles = places[:, None] * freqs[None, :]
    cosine = jnp.cos(angles)[:, None, :]
    sine = jnp.sin(angles)[:, None, :]
    first = vectors[..., :half]
    second = vectors[..., half:]
    return jnp.concatenate([first * cosine - second * sine, first * sine + second * cosine], axis=-1)

def reference(tokens, attn_gain, w_query, w_key, w_value, w_out, prefix_cache, group_of, lengths, moe_gain, w_gate, w_up, w_down, routes, route_weights):
    places = (PREFIX + jnp.arange(SLOTS, dtype=jnp.int32)).astype(jnp.float32)

    def one_request(request):
        rows_in = lax.dynamic_slice_in_dim(tokens, request * SLOTS, SLOTS, 0)
        normed = norm_rows(rows_in, attn_gain).astype(jnp.bfloat16)
        query = jnp.dot(normed, w_query, preferred_element_type=jnp.float32).reshape(SLOTS, HEADS, HD)
        query = rotate(query, places).astype(jnp.bfloat16)
        key = jnp.dot(normed, w_key, preferred_element_type=jnp.float32).reshape(SLOTS, HEADS, HD)
        key = rotate(key, places).astype(jnp.bfloat16)
        value = jnp.dot(normed, w_value, preferred_element_type=jnp.float32).astype(jnp.bfloat16).reshape(SLOTS, HEADS, HD)
        cached = jnp.take(prefix_cache, group_of[request], axis=0)
        keys = jnp.concatenate([cached[:, 0].reshape(PREFIX, HEADS, HD), key], axis=0)
        values = jnp.concatenate([cached[:, 1].reshape(PREFIX, HEADS, HD), value], axis=0)
        scores = jnp.einsum('qhd,khd->hqk', query.astype(jnp.float32), keys.astype(jnp.float32)) / math.sqrt(HD)
        live = jnp.concatenate([jnp.ones((PREFIX,), bool), jnp.arange(SLOTS, dtype=jnp.int32) < lengths[request]])
        scores = jnp.where(live[None, None, :], scores, -1e+30)
        top_score = lax.optimization_barrier(jnp.max(scores, axis=-1, keepdims=True))
        raised = jnp.exp(scores - top_score)
        probs = (raised / lax.optimization_barrier(jnp.sum(raised, axis=-1, keepdims=True))).astype(jnp.bfloat16)
        attn = jnp.einsum('hqk,khd->qhd', probs.astype(jnp.float32), values.astype(jnp.float32)).astype(jnp.bfloat16)
        attn_out = jnp.dot(attn.reshape(SLOTS, HEADS * HD), w_out, preferred_element_type=jnp.float32)
        return (rows_in.astype(jnp.float32) + attn_out).astype(jnp.bfloat16)
    hidden_state = lax.map(one_request, jnp.arange(N_REQ, dtype=jnp.int32)).reshape(ROWS, D)
    normed2 = norm_rows(hidden_state, moe_gain).astype(jnp.bfloat16)
    flat = routes.reshape(-1).astype(jnp.int32)
    order = jnp.argsort(flat, stable=True).astype(jnp.int32)
    sorted_ids = flat[order]
    starts = jnp.searchsorted(sorted_ids, jnp.arange(EXPERTS, dtype=jnp.int32)).astype(jnp.int32)
    ends = jnp.concatenate([starts[1:], jnp.array([ROWS * TOP], dtype=jnp.int32)])
    counts = ends - starts
    most_rows = N_REQ * N_EXP * CAP
    flat_weights = route_weights.reshape(-1)

    def expert_step(total, expert):
        offsets = jnp.arange(most_rows, dtype=jnp.int32)
        valid = offsets < counts[expert]
        index = jnp.minimum(starts[expert] + offsets, ROWS * TOP - 1)
        pair = order[index]
        source = pair // TOP
        rows_in = normed2[source]
        result = jnp.zeros((most_rows, D), jnp.float32)
        for half in range(2):
            gate = jnp.dot(rows_in, w_gate[2 * expert + half], preferred_element_type=jnp.float32)
            upper = jnp.dot(rows_in, w_up[2 * expert + half], preferred_element_type=jnp.float32)
            act = (jax.nn.silu(gate) * upper).astype(jnp.bfloat16)
            result = result + jnp.dot(act, w_down[2 * expert + half], preferred_element_type=jnp.float32)
        part = lax.optimization_barrier(result.astype(jnp.bfloat16))
        scale = jnp.where(valid, flat_weights[pair], 0.0)
        return (total.at[source].add(part.astype(jnp.float32) * scale[:, None]), None)
    moe, _ = lax.scan(expert_step, jnp.zeros((ROWS, D), jnp.float32), jnp.arange(EXPERTS, dtype=jnp.int32))
    slot_index = jnp.arange(ROWS, dtype=jnp.int32)
    live_rows = slot_index % SLOTS < lengths[slot_index // SLOTS]
    return jnp.where(live_rows[:, None], hidden_state.astype(jnp.float32) + moe, 0.0).astype(jnp.bfloat16)
```

```python
import functools
import math

import jax
import jax.numpy as jnp
from jax import lax
from jax.experimental import pallas as pl
from jax.experimental.pallas import tpu as pltpu
from jax.sharding import PartitionSpec as P

HD = 128
PREFIX = 1024
MESH = pl.DeviceIdType.MESH
ANY = pl.BlockSpec(memory_space=pl.ANY)
BOTH = ("req", "exp")


def norm_rows(values, gain):
    wide = values.astype(jnp.float32)
    return wide * lax.rsqrt(jnp.mean(wide * wide, axis=-1, keepdims=True) + 1e-05) * gain


def greet(peers):
    barrier = pltpu.get_barrier_semaphore()
    for peer in peers:
        pl.semaphore_signal(barrier, inc=1, device_id=peer, device_id_type=MESH)
    pl.semaphore_wait(barrier, len(peers))


def remote(src, dst, sems, i, peer):
    return pltpu.make_async_remote_copy(
        src_ref=src,
        dst_ref=dst,
        send_sem=sems.at[0, i],
        recv_sem=sems.at[1, i],
        device_id=peer,
        device_id_type=MESH,
    )


def plane():
    q = lax.axis_index("req")
    z = lax.axis_index("exp")
    core = lax.rem(q, 2)
    x = lax.rem(q // 2, 2)
    y = q // 4
    xn = q + 2 - 4 * x
    yn = q + 4 - 8 * y
    dg = xn + 4 - 8 * y
    other = 1 - 2 * core
    return q, z, xn, yn, dg, other


def first_kernel(nz, nq, tok, pre, tok_out, pre_out, zs, qs, ls):
    q = lax.axis_index("req")
    z = lax.axis_index("exp")
    zp = [(q, lax.rem(z + j, nz)) for j in range(1, nz)]
    qp = [lax.rem(q + j, nq) for j in range(1, nq)]
    greet(zp + [(p, z) for p in qp])
    copies = []
    for i, peer in enumerate(zp):
        c = remote(tok, tok_out.at[z], zs, i, peer)
        c.start()
        copies.append(c)
    for i, p in enumerate(qp):
        c = remote(pre.at[p], pre_out.at[q], qs, i, (p, z))
        c.start()
        copies.append(c)
    for c in (
        pltpu.make_async_copy(tok, tok_out.at[z], ls.at[0]),
        pltpu.make_async_copy(pre.at[q], pre_out.at[q], ls.at[1]),
    ):
        c.start()
        copies.append(c)
    for c in copies:
        c.wait()


def first(tokens, outgoing, nz, nq):
    return pl.pallas_call(
        functools.partial(first_kernel, nz, nq),
        out_shape=(
            jax.ShapeDtypeStruct((nz,) + tokens.shape, tokens.dtype),
            jax.ShapeDtypeStruct(outgoing.shape, outgoing.dtype),
        ),
        in_specs=[ANY, ANY],
        out_specs=(ANY, ANY),
        scratch_shapes=[
            pltpu.SemaphoreType.DMA((2, nz - 1)),
            pltpu.SemaphoreType.DMA((2, nq - 1)),
            pltpu.SemaphoreType.DMA((2,)),
        ],
        compiler_params=pltpu.CompilerParams(collective_id=0, has_side_effects=True),
    )(tokens, outgoing)


def heads_kernel(nz, width, src, dst, zs, ls):
    q = lax.axis_index("req")
    z = lax.axis_index("exp")
    peers = [(q, lax.rem(z + j, nz)) for j in range(1, nz)]
    greet(peers)
    mine = dst.at[:, pl.ds(pl.multiple_of(z * width, width), width)]
    copies = [remote(src, mine, zs, i, peer) for i, peer in enumerate(peers)]
    copies.append(pltpu.make_async_copy(src, mine, ls))
    for c in copies:
        c.start()
    for c in copies:
        c.wait()


def heads(attn, nz):
    rows, width = attn.shape
    return pl.pallas_call(
        functools.partial(heads_kernel, nz, width),
        out_shape=jax.ShapeDtypeStruct((rows, nz * width), attn.dtype),
        in_specs=[ANY],
        out_specs=ANY,
        scratch_shapes=[pltpu.SemaphoreType.DMA((2, nz - 1)), pltpu.SemaphoreType.DMA],
        compiler_params=pltpu.CompilerParams(collective_id=1, has_side_effects=True),
    )(attn)


def attend_kernel(length, tok, gain, wq, wk, wv, cosine, sine, pk, pv, out, normed):
    @pl.when(pl.program_id(0) == 0)
    def _():
        normed[...] = norm_rows(tok[...], gain[...]).astype(jnp.bfloat16)

    def project(w):
        return jnp.dot(normed[...], w[...], preferred_element_type=jnp.float32)

    def rot(v):
        return (v * cosine[...] + pltpu.roll(v, HD // 2, 1) * sine[...]).astype(jnp.bfloat16)

    def across(a, b):
        return lax.dot_general(a, b, (((1,), (1,)), ((), ())), preferred_element_type=jnp.float32)

    query = rot(project(wq))
    key = rot(project(wk))
    value = project(wv).astype(jnp.bfloat16)
    scale = 1.0 / math.sqrt(HD)
    s1 = across(query, pk[...]) * scale
    s2 = across(query, key) * scale
    live = lax.broadcasted_iota(jnp.int32, s2.shape, 1) < length[0]
    s2 = jnp.where(live, s2, -1e30)
    top = jnp.maximum(
        jnp.max(s1, axis=-1, keepdims=True), jnp.max(s2, axis=-1, keepdims=True)
    )
    e1 = jnp.exp(s1 - top)
    e2 = jnp.exp(s2 - top)
    total = jnp.sum(e1, axis=-1, keepdims=True) + jnp.sum(e2, axis=-1, keepdims=True)
    inv = 1.0 / total
    p1 = (e1 * inv).astype(jnp.bfloat16)
    p2 = (e2 * inv).astype(jnp.bfloat16)
    attn = jnp.dot(p1, pv[...], preferred_element_type=jnp.float32)
    attn += jnp.dot(p2, value, preferred_element_type=jnp.float32)
    out[...] = attn.astype(jnp.bfloat16)


def attend(length, tok, gain, wq, wk, wv, cosine, sine, prefix):
    rows, width = tok.shape
    local = wq.shape[1]
    n = local // HD
    whole = lambda a: pl.BlockSpec(a.shape, lambda h, s: (0, 0))
    weight = pl.BlockSpec((width, HD), lambda h, s: (0, h))
    return pl.pallas_call(
        attend_kernel,
        out_shape=jax.ShapeDtypeStruct((rows, local), jnp.bfloat16),
        grid_spec=pltpu.PrefetchScalarGridSpec(
            num_scalar_prefetch=1,
            grid=(n,),
            in_specs=[
                whole(tok),
                whole(gain),
                weight,
                weight,
                weight,
                whole(cosine),
                whole(sine),
                pl.BlockSpec((prefix.shape[0], HD), lambda h, s: (0, h)),
                pl.BlockSpec((prefix.shape[0], HD), lambda h, s: (0, n + h)),
            ],
            out_specs=pl.BlockSpec((rows, HD), lambda h, s: (0, h)),
            scratch_shapes=[pltpu.VMEM((rows, width), jnp.bfloat16)],
        ),
        compiler_params=pltpu.CompilerParams(vmem_limit_bytes=56 * 2**20),
    )(length, tok, gain, wq, wk, wv, cosine, sine, prefix, prefix)


def gather_kernel(src, out, sems, ls):
    q, z, xn, yn, dg, other = plane()
    rows = src.shape[0]
    half = rows // 2
    top, low = pl.ds(0, half), pl.ds(half, half)
    tox, toy, sib = (xn, z), (yn, z), (q + other, z)
    greet([tox, toy, sib])
    own = pltpu.make_async_copy(src, out.at[q], ls)
    x1 = remote(src.at[top], out.at[q, top], sems, 0, tox)
    y1 = remote(src.at[low], out.at[q, low], sems, 1, toy)
    x2 = remote(src.at[low], out.at[q, low], sems, 2, tox)
    y2 = remote(src.at[top], out.at[q, top], sems, 3, toy)
    s0 = remote(src, out.at[q], sems, 4, sib)
    for c in (x1, y1, x2, y2, s0, own):
        c.start()
    y3 = remote(out.at[xn, top], out.at[xn, top], sems, 5, toy)
    x3 = remote(out.at[yn, low], out.at[yn, low], sems, 6, tox)
    hand = [
        remote(out.at[r, part], out.at[r, part], sems, 7 + i, sib)
        for i, (r, part) in enumerate(
            ((xn, top), (yn, low), (xn, low), (yn, top), (dg, top), (dg, low))
        )
    ]
    x1.wait_recv()
    y3.start()
    hand[0].start()
    y1.wait_recv()
    x3.start()
    hand[1].start()
    x2.wait_recv()
    hand[2].start()
    y2.wait_recv()
    hand[3].start()
    y3.wait_recv()
    hand[4].start()
    x3.wait_recv()
    hand[5].start()
    for c in (x1, y1, x2, y2, y3, x3):
        c.wait_send()
    for c in [s0, own] + hand:
        c.wait()


def gather(rows_of, nq):
    return pl.pallas_call(
        gather_kernel,
        out_shape=jax.ShapeDtypeStruct((nq,) + rows_of.shape, rows_of.dtype),
        in_specs=[ANY],
        out_specs=ANY,
        scratch_shapes=[pltpu.SemaphoreType.DMA((2, 13)), pltpu.SemaphoreType.DMA],
        compiler_params=pltpu.CompilerParams(collective_id=2, has_side_effects=True),
    )(rows_of)


def expert_kernel(lengths, x, w, gate, up, down, out):
    rows = x.shape[0]
    start = pl.program_id(1) * rows
    live = start < lengths[pl.program_id(0)]

    @pl.when(live)
    def _():
        g = jnp.dot(x[...], gate[...], preferred_element_type=jnp.float32)
        u = jnp.dot(x[...], up[...], preferred_element_type=jnp.float32)
        act = (g / (1.0 + jnp.exp(-g)) * u).astype(jnp.bfloat16)
        part = jnp.dot(act, down[...], preferred_element_type=jnp.float32)
        out[...] = (part * w[...]).astype(jnp.bfloat16)

    @pl.when(jnp.logical_not(live))
    def _():
        out[...] = jnp.zeros_like(out)


def experts_on(lengths, x, w, gate, up, down, slots):
    count, width = x.shape
    block = 256
    per = slots // block
    fixed = lambda a: pl.BlockSpec(a.shape, lambda r, b, s: (0, 0))
    rows = lambda c: pl.BlockSpec((block, c), lambda r, b, s: (r * per + b, 0))
    return pl.pallas_call(
        expert_kernel,
        out_shape=jax.ShapeDtypeStruct((count, width), jnp.bfloat16),
        grid_spec=pltpu.PrefetchScalarGridSpec(
            num_scalar_prefetch=1,
            grid=(count // slots, per),
            in_specs=[rows(width), rows(1), fixed(gate), fixed(up), fixed(down)],
            out_specs=rows(width),
        ),
        compiler_params=pltpu.CompilerParams(vmem_limit_bytes=56 * 2**20),
    )(lengths, x, w, gate, up, down)


def scatter_kernel(nz, parts, out, held, came, rx, ry, rz, sems, zs, ls):
    q, z, xn, yn, dg, other = plane()
    slots, width = parts.shape[1:]
    half = width // 2
    mine_rows = slots // nz
    left, right = pl.ds(0, half), pl.ds(half, half)
    tox, toy, sib = (xn, z), (yn, z), (q + other, z)
    peers = [lax.rem(z + j, nz) for j in range(1, nz)]
    greet([tox, toy, sib] + [(q, p) for p in peers])
    order = (dg, xn, yn, q)
    DG, XN, YN, ME = range(4)
    swap = [remote(parts.at[r + other], came.at[k], sems, k, sib) for k, r in enumerate(order)]
    load = [pltpu.make_async_copy(parts.at[r], held.at[k], ls.at[k]) for k, r in enumerate(order)]
    for c in swap:
        c.start()
    for c in load:
        c.start()
    step = 64

    def add(dst, src):
        @pl.loop(0, slots // step)
        def _(i):
            at = pl.ds(pl.multiple_of(i * step, step), step)
            dst[at, :] = dst[at, :] + src[at, :]

    x1 = remote(held.at[DG, :, left], rx.at[0], sems, 4, tox)
    y1 = remote(held.at[DG, :, right], ry.at[0], sems, 5, toy)
    x2 = remote(held.at[XN, :, left], rx.at[1], sems, 6, tox)
    y2 = remote(held.at[YN, :, right], ry.at[1], sems, 7, toy)
    x3 = remote(held.at[XN, :, right], rx.at[2], sems, 8, tox)
    y3 = remote(held.at[YN, :, left], ry.at[2], sems, 9, toy)
    for k, after in ((DG, (x1, y1)), (XN, (x2,)), (YN, (y2,)), (ME, ())):
        swap[k].wait_recv()
        load[k].wait()
        add(held.at[k], came.at[k])
        for c in after:
            c.start()
    x1.wait_recv()
    add(held.at[YN, :, left], rx.at[0])
    y3.start()
    y1.wait_recv()
    add(held.at[XN, :, right], ry.at[0])
    x3.start()
    x2.wait_recv()
    add(held.at[ME, :, left], rx.at[1])
    y2.wait_recv()
    add(held.at[ME, :, right], ry.at[1])

    def shard(p, cols):
        return held.at[ME, pl.ds(pl.multiple_of(p * mine_rows, mine_rows), mine_rows), cols]

    sent = []
    for side, cols, c, came_in in ((0, left, y3, ry.at[2]), (1, right, x3, rx.at[2])):
        c.wait_recv()
        add(held.at[ME, :, cols], came_in)
        for i, p in enumerate(peers):
            s = remote(shard(p, cols), rz.at[i, :, cols], zs, side * (nz - 1) + i, (q, p))
            s.start()
            sent.append(s)
    own = shard(z, slice(None))
    for s in sent:
        s.wait()
    total = own[...].astype(jnp.float32)
    for i in range(nz - 1):
        total += rz[i].astype(jnp.float32)
    out[...] = total
    for c in swap + [x1, y1, x2, y2, x3, y3]:
        c.wait_send()


def scatter(parts, nz):
    nq, slots, width = parts.shape
    bf = jnp.bfloat16
    return pl.pallas_call(
        functools.partial(scatter_kernel, nz),
        out_shape=jax.ShapeDtypeStruct((slots // nz, width), jnp.float32),
        in_specs=[ANY],
        out_specs=pl.BlockSpec(memory_space=pltpu.VMEM),
        scratch_shapes=[
            pltpu.VMEM((4, slots, width), bf),
            pltpu.VMEM((4, slots, width), bf),
            pltpu.VMEM((3, slots, width // 2), bf),
            pltpu.VMEM((3, slots, width // 2), bf),
            pltpu.VMEM((nz - 1, slots // nz, width), bf),
            pltpu.SemaphoreType.DMA((2, 10)),
            pltpu.SemaphoreType.DMA((2, 2 * (nz - 1))),
            pltpu.SemaphoreType.DMA((4,)),
        ],
        compiler_params=pltpu.CompilerParams(
            collective_id=3, has_side_effects=True, vmem_limit_bytes=56 * 2**20
        ),
    )(parts)


def on_device(
    tokens,
    attn_gain,
    w_query,
    w_key,
    w_value,
    w_out,
    prefix_cache,
    group_of,
    lengths,
    moe_gain,
    w_gate,
    w_up,
    w_down,
    routes,
    route_weights,
):
    rows_dev, width = tokens.shape
    nz = lax.axis_size("exp")
    nq = lax.axis_size("req")
    z = lax.axis_index("exp")
    q = lax.axis_index("req")
    paths = (nq, nz) == (8, 4)
    local = w_query.shape[1]
    slots = rows_dev * nz
    experts = nq * nz // 2

    groups, piece, _, _ = prefix_cache.shape
    flat_cache = prefix_cache.reshape(groups, piece, 2 * local)
    outgoing = jnp.stack(
        [lax.dynamic_index_in_dim(flat_cache, group_of[r], 0, keepdims=False) for r in range(nq)]
    )
    if paths:
        mine, arrived = first(tokens, outgoing, nz, nq)
    else:
        mine = lax.all_gather(tokens, "exp", axis=0)
        arrived = lax.all_to_all(outgoing, "req", split_axis=0, concat_axis=0, tiled=True)
    mine = mine.reshape(slots, width)
    arrived = arrived.reshape(nq * piece, 2 * local)

    share = w_out.shape[0] // nq
    w_part = lax.dynamic_slice_in_dim(w_out, q * share, share, 0)
    w_whole = lax.all_gather(w_part, ("exp", "req"), axis=0, tiled=True)

    named = routes[:, :, None] == jnp.arange(experts, dtype=jnp.int32)
    dense = jnp.sum(jnp.where(named, route_weights[:, :, None], 0.0), axis=1)
    dense = lax.all_gather(dense, BOTH, axis=0, tiled=True)
    expert = (q * nz + z) // 2
    weight = jnp.sum(
        jnp.where(jnp.arange(experts, dtype=jnp.int32) == expert, dense, 0.0), axis=1, keepdims=True
    )

    half = HD // 2
    freqs = 10000.0 ** (-(jnp.arange(half, dtype=jnp.float32) * 2.0) / HD)
    places = (PREFIX + jnp.arange(slots, dtype=jnp.int32)).astype(jnp.float32)
    angles = places[:, None] * freqs[None, :]
    cosine = jnp.cos(angles)
    sine = jnp.sin(angles)
    cosine = jnp.concatenate([cosine, cosine], axis=1)
    sine = jnp.concatenate([-sine, sine], axis=1)

    length = lax.dynamic_slice_in_dim(lengths, q, 1, 0)
    attn = attend(
        length, mine, attn_gain[None, :], w_query, w_key, w_value, cosine, sine, arrived
    )
    attn = heads(attn, nz) if paths else lax.all_gather(attn, "exp", axis=1, tiled=True)
    attn_out = jnp.dot(attn, w_whole, preferred_element_type=jnp.float32)
    hidden = (mine.astype(jnp.float32) + attn_out).astype(jnp.bfloat16)
    normed2 = norm_rows(hidden, moe_gain).astype(jnp.bfloat16)
    if paths:
        every = gather(normed2, nq).reshape(nq * slots, width)
    else:
        every = lax.all_gather(normed2, "req", axis=0, tiled=True)
    parts = experts_on(lengths, every, weight, w_gate[0], w_up[0], w_down[0], slots)
    if paths:
        moe = scatter(parts.reshape(nq, slots, width), nz)
    else:
        moe = lax.psum_scatter(parts, "req", scatter_dimension=0, tiled=True)
        moe = lax.psum_scatter(moe, "exp", scatter_dimension=0, tiled=True).astype(jnp.float32)
    own = lax.dynamic_slice_in_dim(hidden, z * rows_dev, rows_dev, 0)
    place = z * rows_dev + jnp.arange(rows_dev, dtype=jnp.int32)
    return jnp.where((place < length)[:, None], own.astype(jnp.float32) + moe, 0.0).astype(
        jnp.bfloat16
    )


def solution(mesh):
    spread = P(BOTH, None, None)
    return jax.shard_map(
        on_device,
        mesh=mesh,
        in_specs=(
            P(BOTH, None),
            P(),
            P(None, "exp"),
            P(None, "exp"),
            P(None, "exp"),
            P("exp", None),
            P(None, "req", None, "exp"),
            P(),
            P(),
            P(),
            spread,
            spread,
            spread,
            P(BOTH, None),
            P(BOTH, None),
        ),
        out_specs=P(BOTH, None),
        check_vma=False,
    )
```

```python
import functools
import math

import jax
import jax.numpy as jnp
from jax import lax
from jax.experimental import pallas as pl
from jax.experimental.pallas import tpu as pltpu
from jax.sharding import PartitionSpec as P

HD = 128
PREFIX = 1024
MESH = pl.DeviceIdType.MESH
ANY = pl.BlockSpec(memory_space=pl.ANY)
BOTH = ("req", "exp")


def norm_rows(values, gain):
    wide = values.astype(jnp.float32)
    return wide * lax.rsqrt(jnp.mean(wide * wide, axis=-1, keepdims=True) + 1e-05) * gain


def greet(peers):
    barrier = pltpu.get_barrier_semaphore()
    for peer in peers:
        pl.semaphore_signal(barrier, inc=1, device_id=peer, device_id_type=MESH)
    pl.semaphore_wait(barrier, len(peers))


def remote(src, dst, sems, i, peer):
    return pltpu.make_async_remote_copy(
        src_ref=src,
        dst_ref=dst,
        send_sem=sems.at[0, i],
        recv_sem=sems.at[1, i],
        device_id=peer,
        device_id_type=MESH,
    )


def plane():
    q = lax.axis_index("req")
    z = lax.axis_index("exp")
    core = lax.rem(q, 2)
    x = lax.rem(q // 2, 2)
    y = q // 4
    xn = q + 2 - 4 * x
    yn = q + 4 - 8 * y
    dg = xn + 4 - 8 * y
    other = 1 - 2 * core
    return q, z, xn, yn, dg, other


def choose_kernel(groups, src, dst):
    dst[...] = src[...]


def choose(group_of, cache):
    block = (1,) + cache.shape[1:]
    return pl.pallas_call(
        choose_kernel,
        out_shape=jax.ShapeDtypeStruct(group_of.shape + cache.shape[1:], cache.dtype),
        grid_spec=pltpu.PrefetchScalarGridSpec(
            num_scalar_prefetch=1,
            grid=group_of.shape,
            in_specs=[pl.BlockSpec(block, lambda r, g: (g[r], 0, 0))],
            out_specs=pl.BlockSpec(block, lambda r, g: (r, 0, 0)),
        ),
    )(group_of, cache)


def first_kernel(nz, nq, tok, pre, wts, tok_out, pre_out, wts_out, zs, qs, ws, vs, ls):
    q = lax.axis_index("req")
    z = lax.axis_index("exp")
    zp = [(q, lax.rem(z + j, nz)) for j in range(1, nz)]
    qp = [lax.rem(q + j, nq) for j in range(1, nq)]
    greet(zp + [(p, z) for p in qp])
    copies = [
        pltpu.make_async_copy(wts, wts_out.at[q, z], ls.at[2]),
        pltpu.make_async_copy(tok, tok_out.at[z], ls.at[0]),
        pltpu.make_async_copy(pre.at[q], pre_out.at[q], ls.at[1]),
    ]
    gathers = [remote(wts, wts_out.at[q, z], ws, i, peer) for i, peer in enumerate(zp)]
    copies += [remote(tok, tok_out.at[z], zs, i, peer) for i, peer in enumerate(zp)]
    copies += [remote(pre.at[p], pre_out.at[q], qs, i, (p, z)) for i, p in enumerate(qp)]
    for c in gathers + copies:
        c.start()
    for c in gathers:
        c.wait()
    copies[0].wait()
    passed = [remote(wts_out.at[q], wts_out.at[q], vs, i, (p, z)) for i, p in enumerate(qp)]
    for c in passed:
        c.start()
    for c in copies[1:] + passed:
        c.wait()


def first(tokens, outgoing, weights, nz, nq):
    return pl.pallas_call(
        functools.partial(first_kernel, nz, nq),
        out_shape=(
            jax.ShapeDtypeStruct((nz,) + tokens.shape, tokens.dtype),
            jax.ShapeDtypeStruct(outgoing.shape, outgoing.dtype),
            jax.ShapeDtypeStruct((nq, nz) + weights.shape, weights.dtype),
        ),
        in_specs=[ANY, ANY, ANY],
        out_specs=(ANY, ANY, ANY),
        scratch_shapes=[
            pltpu.SemaphoreType.DMA((2, nz - 1)),
            pltpu.SemaphoreType.DMA((2, nq - 1)),
            pltpu.SemaphoreType.DMA((2, nz - 1)),
            pltpu.SemaphoreType.DMA((2, nq - 1)),
            pltpu.SemaphoreType.DMA((3,)),
        ],
        compiler_params=pltpu.CompilerParams(collective_id=0, has_side_effects=True),
    )(tokens, outgoing, weights)


def heads_kernel(nz, src, dst, zs, ls):
    q = lax.axis_index("req")
    z = lax.axis_index("exp")
    peers = [(q, lax.rem(z + j, nz)) for j in range(1, nz)]
    greet(peers)
    mine = dst.at[z]
    copies = [remote(src, mine, zs, i, peer) for i, peer in enumerate(peers)]
    copies.append(pltpu.make_async_copy(src, mine, ls))
    for c in copies:
        c.start()
    for c in copies:
        c.wait()


def heads(attn, nz):
    return pl.pallas_call(
        functools.partial(heads_kernel, nz),
        out_shape=jax.ShapeDtypeStruct((nz,) + attn.shape, attn.dtype),
        in_specs=[ANY],
        out_specs=ANY,
        scratch_shapes=[pltpu.SemaphoreType.DMA((2, nz - 1)), pltpu.SemaphoreType.DMA],
        compiler_params=pltpu.CompilerParams(collective_id=1, has_side_effects=True),
    )(attn)


def attend_kernel(length, tok, gain, wq, wk, wv, cosine, sine, pk, pv, out, normed):
    @pl.when(pl.program_id(0) == 0)
    def _():
        normed[...] = norm_rows(tok[...], gain[...]).astype(jnp.bfloat16)

    def project(w):
        return jnp.dot(normed[...], w[...], preferred_element_type=jnp.float32)

    def rot(v):
        return (v * cosine[...] + pltpu.roll(v, HD // 2, 1) * sine[...]).astype(jnp.bfloat16)

    def across(a, b):
        return lax.dot_general(a, b, (((1,), (1,)), ((), ())), preferred_element_type=jnp.float32)

    query = rot(project(wq))
    key = rot(project(wk))
    value = project(wv).astype(jnp.bfloat16)
    scale = 1.0 / math.sqrt(HD)
    s1 = across(query, pk[...]) * scale
    s2 = across(query, key) * scale
    live = lax.broadcasted_iota(jnp.int32, s2.shape, 1) < length[0]
    s2 = jnp.where(live, s2, -1e30)
    top = jnp.maximum(
        jnp.max(s1, axis=-1, keepdims=True), jnp.max(s2, axis=-1, keepdims=True)
    )
    e1 = jnp.exp(s1 - top)
    e2 = jnp.exp(s2 - top)
    total = jnp.sum(e1, axis=-1, keepdims=True) + jnp.sum(e2, axis=-1, keepdims=True)
    inv = 1.0 / total
    p1 = (e1 * inv).astype(jnp.bfloat16)
    p2 = (e2 * inv).astype(jnp.bfloat16)
    attn = jnp.dot(p1, pv[...], preferred_element_type=jnp.float32)
    attn += jnp.dot(p2, value, preferred_element_type=jnp.float32)
    out[...] = attn.astype(jnp.bfloat16)


def attend(length, tok, gain, wq, wk, wv, cosine, sine, prefix):
    rows, width = tok.shape
    local = wq.shape[1]
    n = local // HD
    whole = lambda a: pl.BlockSpec(a.shape, lambda h, s: (0, 0))
    weight = pl.BlockSpec((width, HD), lambda h, s: (0, h))
    return pl.pallas_call(
        attend_kernel,
        out_shape=jax.ShapeDtypeStruct((rows, local), jnp.bfloat16),
        grid_spec=pltpu.PrefetchScalarGridSpec(
            num_scalar_prefetch=1,
            grid=(n,),
            in_specs=[
                whole(tok),
                whole(gain),
                weight,
                weight,
                weight,
                whole(cosine),
                whole(sine),
                pl.BlockSpec((prefix.shape[0], HD), lambda h, s: (0, h)),
                pl.BlockSpec((prefix.shape[0], HD), lambda h, s: (0, n + h)),
            ],
            out_specs=pl.BlockSpec((rows, HD), lambda h, s: (0, h)),
            scratch_shapes=[pltpu.VMEM((rows, width), jnp.bfloat16)],
        ),
        compiler_params=pltpu.CompilerParams(vmem_limit_bytes=56 * 2**20),
    )(length, tok, gain, wq, wk, wv, cosine, sine, prefix, prefix)


def gather_kernel(src, out, sems, ls):
    q, z, xn, yn, dg, other = plane()
    rows = src.shape[0]
    half = rows // 2
    top, low = pl.ds(0, half), pl.ds(half, half)
    tox, toy, sib = (xn, z), (yn, z), (q + other, z)
    greet([tox, toy, sib])
    own = pltpu.make_async_copy(src, out.at[q], ls)
    x1 = remote(src.at[top], out.at[q, top], sems, 0, tox)
    y1 = remote(src.at[low], out.at[q, low], sems, 1, toy)
    x2 = remote(src.at[low], out.at[q, low], sems, 2, tox)
    y2 = remote(src.at[top], out.at[q, top], sems, 3, toy)
    s0 = remote(src, out.at[q], sems, 4, sib)
    for c in (x1, y1, x2, y2, s0, own):
        c.start()
    y3 = remote(out.at[xn, top], out.at[xn, top], sems, 5, toy)
    x3 = remote(out.at[yn, low], out.at[yn, low], sems, 6, tox)
    hand = [
        remote(out.at[r, part], out.at[r, part], sems, 7 + i, sib)
        for i, (r, part) in enumerate(
            ((xn, top), (yn, low), (xn, low), (yn, top), (dg, top), (dg, low))
        )
    ]
    x1.wait_recv()
    y3.start()
    hand[0].start()
    y1.wait_recv()
    x3.start()
    hand[1].start()
    x2.wait_recv()
    hand[2].start()
    y2.wait_recv()
    hand[3].start()
    y3.wait_recv()
    hand[4].start()
    x3.wait_recv()
    hand[5].start()
    for c in (x1, y1, x2, y2, y3, x3):
        c.wait_send()
    for c in [s0, own] + hand:
        c.wait()


def gather(rows_of, nq):
    return pl.pallas_call(
        gather_kernel,
        out_shape=jax.ShapeDtypeStruct((nq,) + rows_of.shape, rows_of.dtype),
        in_specs=[ANY],
        out_specs=ANY,
        scratch_shapes=[pltpu.SemaphoreType.DMA((2, 13)), pltpu.SemaphoreType.DMA],
        compiler_params=pltpu.CompilerParams(collective_id=2, has_side_effects=True),
    )(rows_of)


def expert_kernel(lengths, x, w, gate, up, down, out):
    rows = x.shape[0]
    start = pl.program_id(1) * rows
    live = start < lengths[pl.program_id(0)]

    @pl.when(live)
    def _():
        g = jnp.dot(x[...], gate[...], preferred_element_type=jnp.float32)
        u = jnp.dot(x[...], up[...], preferred_element_type=jnp.float32)
        act = (g / (1.0 + jnp.exp(-g)) * u).astype(jnp.bfloat16)
        part = jnp.dot(act, down[...], preferred_element_type=jnp.float32)
        out[...] = (part * w[...]).astype(jnp.bfloat16)

    @pl.when(jnp.logical_not(live))
    def _():
        out[...] = jnp.zeros_like(out)


def experts_on(lengths, x, w, gate, up, down, slots):
    count, width = x.shape
    block = 256
    per = slots // block
    fixed = lambda a: pl.BlockSpec(a.shape, lambda r, b, s: (0, 0))
    rows = lambda c: pl.BlockSpec((block, c), lambda r, b, s: (r * per + b, 0))
    return pl.pallas_call(
        expert_kernel,
        out_shape=jax.ShapeDtypeStruct((count, width), jnp.bfloat16),
        grid_spec=pltpu.PrefetchScalarGridSpec(
            num_scalar_prefetch=1,
            grid=(count // slots, per),
            in_specs=[rows(width), rows(1), fixed(gate), fixed(up), fixed(down)],
            out_specs=rows(width),
        ),
        compiler_params=pltpu.CompilerParams(vmem_limit_bytes=56 * 2**20),
    )(lengths, x, w, gate, up, down)


def scatter_kernel(nz, chunks, parts, out, held, came, rx, ry, rz, sems, zs, ls):
    q, z, xn, yn, dg, other = plane()
    slots, width = parts.shape[1:]
    chunk = width // chunks
    half = chunk // 2
    mine_rows = slots // nz
    tox, toy, sib = (xn, z), (yn, z), (q + other, z)
    peers = [lax.rem(z + j, nz) for j in range(1, nz)]
    greet([tox, toy, sib] + [(q, p) for p in peers])
    order = (dg, xn, yn, q)
    DG, XN, YN, ME = range(4)
    step = 128

    def add(dst, src):
        @pl.loop(0, slots // step)
        def _(i):
            at = pl.ds(pl.multiple_of(i * step, step), step)
            dst[at, :] = dst[at, :] + src[at, :]

    class Part:
        pass

    def describe(n):
        p = Part()
        p.cols = pl.ds(n * chunk, chunk)
        left, right = pl.ds(n * chunk, half), pl.ds(n * chunk + half, half)
        p.left, p.right = left, right
        spot = pl.ds(n * half, half)
        p.rx = [rx.at[i, :, spot] for i in range(3)]
        p.ry = [ry.at[i, :, spot] for i in range(3)]
        at = sems.at[n]
        p.swap = [
            remote(parts.at[r + other, :, p.cols], came.at[k, :, p.cols], at, k, sib)
            for k, r in enumerate(order)
        ]
        p.load = [
            pltpu.make_async_copy(parts.at[r, :, p.cols], held.at[k, :, p.cols], ls.at[n, k])
            for k, r in enumerate(order)
        ]
        p.x1 = remote(held.at[DG, :, left], p.rx[0], at, 4, tox)
        p.y1 = remote(held.at[DG, :, right], p.ry[0], at, 5, toy)
        p.x2 = remote(held.at[XN, :, left], p.rx[1], at, 6, tox)
        p.y2 = remote(held.at[YN, :, right], p.ry[1], at, 7, toy)
        p.x3 = remote(held.at[XN, :, right], p.rx[2], at, 8, tox)
        p.y3 = remote(held.at[YN, :, left], p.ry[2], at, 9, toy)
        p.last = [
            remote(
                held.at[ME, pl.ds(pl.multiple_of(d * mine_rows, mine_rows), mine_rows), p.cols],
                rz.at[i, :, p.cols],
                zs.at[n],
                i,
                (q, d),
            )
            for i, d in enumerate(peers)
        ]
        return p

    def cores(p):
        for k, after in ((DG, (p.x1, p.y1)), (XN, (p.x2,)), (YN, (p.y2,)), (ME, ())):
            p.swap[k].wait_recv()
            p.load[k].wait()
            add(held.at[k, :, p.cols], came.at[k, :, p.cols])
            for c in after:
                c.start()

    def turn(p):
        p.x1.wait_recv()
        add(held.at[YN, :, p.left], p.rx[0])
        p.y3.start()
        p.y1.wait_recv()
        add(held.at[XN, :, p.right], p.ry[0])
        p.x3.start()

    def finish(p):
        p.x2.wait_recv()
        add(held.at[ME, :, p.left], p.rx[1])
        p.y2.wait_recv()
        add(held.at[ME, :, p.right], p.ry[1])
        p.y3.wait_recv()
        add(held.at[ME, :, p.left], p.ry[2])
        p.x3.wait_recv()
        add(held.at[ME, :, p.right], p.rx[2])
        for c in p.last:
            c.start()

    pieces = [describe(n) for n in range(chunks)]
    for p in pieces:
        for c in p.swap + p.load:
            c.start()
    for n in range(chunks + 2):
        if n < chunks:
            cores(pieces[n])
        if 1 <= n <= chunks:
            turn(pieces[n - 1])
        if n >= 2:
            finish(pieces[n - 2])
    own = pl.ds(pl.multiple_of(z * mine_rows, mine_rows), mine_rows)
    for p in pieces:
        for c in p.last:
            c.wait()
        total = held[ME, own, p.cols].astype(jnp.float32)
        for i in range(nz - 1):
            total += rz[i, :, p.cols].astype(jnp.float32)
        out[:, p.cols] = total
        for c in p.swap + [p.x1, p.y1, p.x2, p.y2, p.x3, p.y3]:
            c.wait_send()


def scatter(parts, nz):
    nq, slots, width = parts.shape
    bf = jnp.bfloat16
    chunks = 4
    return pl.pallas_call(
        functools.partial(scatter_kernel, nz, chunks),
        out_shape=jax.ShapeDtypeStruct((slots // nz, width), jnp.float32),
        in_specs=[ANY],
        out_specs=pl.BlockSpec(memory_space=pltpu.VMEM),
        scratch_shapes=[
            pltpu.VMEM((4, slots, width), bf),
            pltpu.VMEM((4, slots, width), bf),
            pltpu.VMEM((3, slots, width // 2), bf),
            pltpu.VMEM((3, slots, width // 2), bf),
            pltpu.VMEM((nz - 1, slots // nz, width), bf),
            pltpu.SemaphoreType.DMA((chunks, 2, 10)),
            pltpu.SemaphoreType.DMA((chunks, 2, nz - 1)),
            pltpu.SemaphoreType.DMA((chunks, 4)),
        ],
        compiler_params=pltpu.CompilerParams(
            collective_id=3, has_side_effects=True, vmem_limit_bytes=56 * 2**20
        ),
    )(parts)


def on_device(
    tokens,
    attn_gain,
    w_query,
    w_key,
    w_value,
    w_out,
    prefix_cache,
    group_of,
    lengths,
    moe_gain,
    w_gate,
    w_up,
    w_down,
    routes,
    route_weights,
):
    rows_dev, width = tokens.shape
    nz = lax.axis_size("exp")
    nq = lax.axis_size("req")
    z = lax.axis_index("exp")
    q = lax.axis_index("req")
    paths = (nq, nz) == (8, 4)
    local = w_query.shape[1]
    slots = rows_dev * nz
    experts = nq * nz // 2

    groups, piece, _, _ = prefix_cache.shape
    flat_cache = prefix_cache.reshape(groups, piece, 2 * local)
    outgoing = choose(group_of, flat_cache)
    named = jnp.arange(experts, dtype=jnp.int32)[:, None, None] == routes.T[None]
    dense = jnp.sum(jnp.where(named, route_weights.T[None], 0.0), axis=1)
    if paths:
        mine, arrived, every_weight = first(tokens, outgoing, dense, nz, nq)
    else:
        mine = lax.all_gather(tokens, "exp", axis=0)
        every_weight = lax.all_gather(dense, BOTH, axis=0).reshape(nq, nz, experts, rows_dev)
        arrived = lax.all_to_all(outgoing, "req", split_axis=0, concat_axis=0, tiled=True)
    mine = mine.reshape(slots, width)
    arrived = arrived.reshape(nq * piece, 2 * local)

    share = w_out.shape[0] // nq
    w_part = lax.dynamic_slice_in_dim(w_out, q * share, share, 0)
    w_whole = lax.all_gather(w_part, ("exp", "req"), axis=0, tiled=True)

    expert = (q * nz + z) // 2
    every_weight = lax.dynamic_index_in_dim(every_weight, expert, 2, keepdims=False)
    weight = every_weight.reshape(nq * slots, 1)

    half = HD // 2
    freqs = 10000.0 ** (-(jnp.arange(half, dtype=jnp.float32) * 2.0) / HD)
    places = (PREFIX + jnp.arange(slots, dtype=jnp.int32)).astype(jnp.float32)
    angles = places[:, None] * freqs[None, :]
    cosine = jnp.cos(angles)
    sine = jnp.sin(angles)
    cosine = jnp.concatenate([cosine, cosine], axis=1)
    sine = jnp.concatenate([-sine, sine], axis=1)

    length = lax.dynamic_slice_in_dim(lengths, q, 1, 0)
    attn = attend(
        length, mine, attn_gain[None, :], w_query, w_key, w_value, cosine, sine, arrived
    )
    attn = heads(attn, nz) if paths else lax.all_gather(attn, "exp", axis=0)
    attn = jnp.moveaxis(attn, 0, 1).reshape(slots, nz * local)
    attn_out = jnp.dot(attn, w_whole, preferred_element_type=jnp.float32)
    hidden = (mine.astype(jnp.float32) + attn_out).astype(jnp.bfloat16)
    normed2 = norm_rows(hidden, moe_gain).astype(jnp.bfloat16)
    if paths:
        every = gather(normed2, nq).reshape(nq * slots, width)
    else:
        every = lax.all_gather(normed2, "req", axis=0, tiled=True)
    parts = experts_on(lengths, every, weight, w_gate[0], w_up[0], w_down[0], slots)
    if paths:
        moe = scatter(parts.reshape(nq, slots, width), nz)
    else:
        moe = lax.psum_scatter(parts, "req", scatter_dimension=0, tiled=True)
        moe = lax.psum_scatter(moe, "exp", scatter_dimension=0, tiled=True).astype(jnp.float32)
    own = lax.dynamic_slice_in_dim(hidden, z * rows_dev, rows_dev, 0)
    place = z * rows_dev + jnp.arange(rows_dev, dtype=jnp.int32)
    return jnp.where((place < length)[:, None], own.astype(jnp.float32) + moe, 0.0).astype(
        jnp.bfloat16
    )


def solution(mesh):
    spread = P(BOTH, None, None)
    return jax.shard_map(
        on_device,
        mesh=mesh,
        in_specs=(
            P(BOTH, None),
            P(),
            P(None, "exp"),
            P(None, "exp"),
            P(None, "exp"),
            P("exp", None),
            P(None, "req", None, "exp"),
            P(),
            P(),
            P(),
            spread,
            spread,
            spread,
            P(BOTH, None),
            P(BOTH, None),
        ),
        out_specs=P(BOTH, None),
        check_vma=False,
    )
```
